32 devices in a mesh: section: 2 (over x), fsdp: 16 (over z, y, core).
Axes of the slice: x: 2, y: 2, z: 4, core: 2. Of those that a mesh axis runs over, the one named last changes fastest.
Arguments:
- activations: bfloat16 [2560, 6144], P('fsdp'), may hold values from -36 to 36
- keep: int32 [2560], P('fsdp'), may hold values from 0 to 1, as said below
- gains: bfloat16 [2, 6144], P('section'), may hold values from 0.099609375 to 1.8984375
- up_rows: int32 [2, 192, 2], P('section'), may hold values from 0 to 95
- up_blocks: bfloat16 [2, 384, 4096], P('section', 'fsdp'), may hold values from -0.5 to 0.5
- down_rows: int32 [2, 96, 2], P('section'), may hold values from 0 to 191
- down_blocks: bfloat16 [2, 192, 4096], P('section', 'fsdp'), may hold values from -0.5 to 0.5
Outputs:
- section_out: bfloat16 [2, 2560, 6144], P('section', 'fsdp')
The draws below stay inside these ranges and needn't reach their ends.
Inputs may be any that keep to these rules, and one draw needn't show every extreme that they name: `keep`: each aligned block of 160 tokens (the tokens of one index of fsdp) holds exactly 128 ones.
All inputs are finite; a program needn't handle non-finite values.
Results may differ from the reference program's by a relative error of at most 0.012.
Values may be sent and summed in bfloat16 or wider, within the bound.
A program may use at most 128 MiB of HBM per device.

```python
import math
import jax
import jax.numpy as jnp
from jax import lax

D = 6144
FF = 12288
BLK = 64
UP_DEPTH = 2
DOWN_DEPTH = 2
KEEP_DEV = 128
TOK_DEV = 160
TOKENS = 2560
LAYERS = 2
N_FSDP = 16


def draw_activations(key, part):
    first, second, third = jax.random.split(key, 3)
    row_scale = 0.3 * jnp.exp(jax.random.uniform(second, (TOKENS, 1), jnp.float32) * math.log(10.0))
    col_scale = 0.3 * jnp.exp(jax.random.uniform(third, (1, D), jnp.float32) * math.log(10.0))
    base = jax.random.truncated_normal(first, -4.0, 4.0, (TOKENS, D), jnp.float32)
    return (base * row_scale * col_scale).astype(jnp.bfloat16)


def draw_keep(key, part):
    groups = TOKENS // TOK_DEV
    keys = jax.random.split(key, groups)
    orders = jax.vmap(lambda single: jax.random.permutation(single, TOK_DEV))(keys)
    return (orders < KEEP_DEV).astype(jnp.int32).reshape(TOKENS)


def butterfly_rows(key, columns, rows, depth):
    ratio = max(rows // columns, 1)
    strides = list(range(min(ratio, depth - 1)))
    reach = ratio
    while len(strides) < depth - 1:
        strides.append(reach)
        reach = reach * 2
    first, second = jax.random.split(key)
    offset = jax.random.randint(first, (LAYERS, 1, 1), 0, rows)
    shared = jax.random.randint(second, (LAYERS, 1, 1), 0, rows)
    base = (jnp.arange(columns, dtype=jnp.int32) * rows // columns)[None, :, None]
    band = (base + offset + jnp.array(strides, jnp.int32)[None, None, :]) % rows
    shared = jnp.broadcast_to(shared, (LAYERS, columns, 1))
    return jnp.concatenate([band, shared], axis=2).astype(jnp.int32)


def draw_up_rows(key, part):
    return butterfly_rows(jax.random.fold_in(key, 11), FF // BLK, D // BLK, UP_DEPTH)


def draw_down_rows(key, part):
    return butterfly_rows(jax.random.fold_in(key, 23), D // BLK, FF // BLK, DOWN_DEPTH)


def block_scale(stream_key, dims, cuts, least, high):
    loudness, own = 1.0, jax.random.fold_in(stream_key, 6)
    for dim, parts in cuts:
        heights = jnp.exp(jax.random.uniform(jax.random.fold_in(own, dim), (parts,), jnp.float32, least / len(cuts), high / len(cuts)))
        loudness = loudness * jnp.repeat(heights, dims[dim] // parts).reshape([-1 if axis == dim else 1 for axis in range(len(dims))])
    return loudness


def scatter_about(own_key, shape, deviation, limit, pieces=(), kind=jnp.bfloat16):
    entries = jax.random.normal(own_key, shape, jnp.float32) * deviation
    if len(pieces) > 0:
        entries = block_scale(own_key, shape, pieces, -0.22, 0.18) * entries
    return jnp.clip(entries, min=-limit, max=limit).astype(kind)


def setup_inputs(seed: int = 0) -> dict:
    splits = jax.random.split(jax.random.key(seed), 8)
    return {
        "activations": draw_activations(jax.random.fold_in(splits[7], 71), 0),
        "keep": draw_keep(jax.random.fold_in(splits[7], 71), 0),
        "gains": jnp.clip(1.0 + 0.18 * jax.random.normal(splits[2], (LAYERS, D), jnp.float32), 0.099609375, 1.8984375).astype(jnp.bfloat16),
        "up_rows": draw_up_rows(jax.random.fold_in(splits[7], 71), 0),
        "up_blocks": scatter_about(splits[4], (LAYERS, (FF // BLK) * UP_DEPTH, BLK * BLK), (UP_DEPTH * BLK) ** -0.5, 0.5, ((0, 2), (1, 16))),
        "down_rows": draw_down_rows(jax.random.fold_in(splits[7], 71), 0),
        "down_blocks": scatter_about(splits[6], (LAYERS, (D // BLK) * DOWN_DEPTH, BLK * BLK), (DOWN_DEPTH * BLK) ** -0.5, 0.5, ((0, 2), (1, 16))),
    }


def apply_layer(carried, gain, up_index, up_values, down_index, down_values):
    count = carried.shape[0]
    blocks_in = D // BLK
    blocks_hid = FF // BLK
    wide = carried.astype(jnp.float32)
    meansq = lax.optimization_barrier(jnp.mean(wide * wide, axis=-1, keepdims=True))
    normed = (wide * lax.rsqrt(meansq + 1e-05) * gain.astype(jnp.float32)).astype(jnp.bfloat16)
    picked = normed.reshape(count, blocks_in, BLK)[:, up_index.reshape(-1).astype(jnp.int32), :]
    picked = picked.reshape(count, blocks_hid, UP_DEPTH * BLK)
    weights_up = up_values.reshape(blocks_hid, UP_DEPTH * BLK, BLK)
    up_sums = jnp.einsum('ncr,crj->ncj', picked.astype(jnp.float32), weights_up.astype(jnp.float32))
    hidden = jax.nn.gelu(up_sums, approximate=True).astype(jnp.bfloat16).reshape(count, FF)
    second = hidden.reshape(count, blocks_hid, BLK)[:, down_index.reshape(-1).astype(jnp.int32), :]
    second = second.reshape(count, blocks_in, DOWN_DEPTH * BLK)
    weights_down = down_values.reshape(blocks_in, DOWN_DEPTH * BLK, BLK)
    down_sums = jnp.einsum('ncr,crj->ncj', second.astype(jnp.float32), weights_down.astype(jnp.float32))
    return down_sums.reshape(count, D)

def reference(activations, keep, gains, up_rows, up_blocks, down_rows, down_blocks):
    kept_total = KEEP_DEV * N_FSDP
    chosen = jnp.nonzero(keep, size=kept_total)[0].astype(jnp.int32)
    carried = activations[chosen]
    results = []
    for layer in range(LAYERS):
        branch = apply_layer(carried, gains[layer], up_rows[layer], up_blocks[layer], down_rows[layer], down_blocks[layer])
        carried = (carried.astype(jnp.float32) + branch).astype(jnp.bfloat16)
        results.append(activations.at[chosen].set(carried))
    return jnp.stack(results)
```

```python
import functools
import jax
import jax.numpy as jnp
from jax import lax
from jax.experimental import pallas as pl
from jax.experimental.pallas import tpu as pltpu
from jax.sharding import PartitionSpec as P

BLK = 64
UP_DEPTH = 2
DOWN_DEPTH = 2


def project(source, index, weights):
    count = source.shape[0]

    def one(column, sums):
        first = lax.dynamic_slice_in_dim(source, index[2 * column] * BLK, BLK, 1)
        second = lax.dynamic_slice_in_dim(source, index[2 * column + 1] * BLK, BLK, 1)
        part = jnp.dot(
            jnp.concatenate([first, second], axis=1),
            lax.dynamic_index_in_dim(weights, column, 0, keepdims=False),
            preferred_element_type=jnp.float32,
        )
        return lax.dynamic_update_slice_in_dim(sums, part, column * BLK, 1)

    columns = weights.shape[0]
    return lax.fori_loop(0, columns, one, jnp.zeros((count, columns * BLK), jnp.float32))


def per_device(activations, keep, gains, up_rows, up_blocks, down_rows, down_blocks):
    up_all = lax.all_gather(up_blocks[0], "fsdp", axis=0, tiled=True)
    down_all = lax.all_gather(down_blocks[0], "fsdp", axis=0, tiled=True)
    weights_up = up_all.reshape(-1, UP_DEPTH * BLK, BLK)
    weights_down = down_all.reshape(-1, DOWN_DEPTH * BLK, BLK)
    gain_wide = gains[0].astype(jnp.float32)
    keep_wide = keep.astype(jnp.float32)[:, None]
    section = lax.axis_index("section")
    sections = lax.axis_size("section")

    def turn_step(turn, carry):
        held, record = carry
        wide = held.astype(jnp.float32)
        meansq = jnp.mean(wide * wide, axis=-1, keepdims=True)
        normed = (wide * lax.rsqrt(meansq + 1e-05) * gain_wide).astype(jnp.bfloat16)
        up_sums = project(normed, up_rows[0].reshape(-1), weights_up)
        hidden = jax.nn.gelu(up_sums, approximate=True).astype(jnp.bfloat16)
        down_sums = project(hidden, down_rows[0].reshape(-1), weights_down)
        result = (wide + keep_wide * down_sums).astype(jnp.bfloat16)
        record = jnp.where(section == turn, result, record)
        pairs = [(source, source + 1) for source in range(sections - 1)]
        return lax.ppermute(result, "section", pairs), record

    return lax.fori_loop(0, sections, turn_step, (activations, activations))[1][None]


LANES = 2 * BLK
MESH = pl.DeviceIdType.MESH
RING, SIB, ACROSS = 0, 1, 2


def kernel(
    chips,
    x_ref,
    keep_ref,
    gain_ref,
    rows_ref,
    w_ref,
    out_ref,
    weights,
    blocks_in,
    blocks_hid,
    scale_ref,
    gains,
    rows_in,
    rows,
    send_sem,
    recv_sem,
    small_send,
    small_recv,
    local_sem,
):
    section = lax.axis_index("section")
    me = lax.axis_index("fsdp")
    core = me % 2
    chip = me // 2
    depth_z = chips // 2
    y = chip % 2
    z = chip // 2
    place = z * (1 - y) + (chips - 1 - z) * y
    step_dir = 1 - 2 * core

    def at(position, which):
        position = (position + 2 * chips) % chips
        back = position // depth_z
        zz = position * (1 - back) + (chips - 1 - position) * back
        return (zz * 2 + back) * 2 + which

    ahead = at(place + step_dir, core)
    behind = at(place - step_dir, core)
    sibling = me + 1 - 2 * core
    other = 1 - section
    tokens, width = x_ref.shape
    tiles = width // LANES
    ups = 6 * w_ref.shape[0] // 9
    part = w_ref.shape[0] // 3

    barrier = pltpu.get_barrier_semaphore()
    for device in ((section, ahead), (section, behind), (section, sibling), (other, me)):
        pl.semaphore_signal(barrier, inc=1, device_id=device, device_id_type=MESH)
    pl.semaphore_wait(barrier, 4)

    def origin(step):
        return at(place - step_dir * step, core)

    def origin_sib(step):
        return at(place + step_dir * step, 1 - core)

    def slot(layer, who, piece):
        return weights.at[layer, who, pl.ds(piece * part, part)]

    def send(layer, step, piece, way, own=False):
        who = origin(step)
        device = ((section, ahead), (section, sibling), (other, me))[way]
        return pltpu.make_async_remote_copy(
            src_ref=w_ref.at[pl.ds(piece * part, part)] if own else slot(layer, who, piece),
            dst_ref=slot(layer, who, piece),
            send_sem=send_sem.at[layer, step, piece, way],
            recv_sem=recv_sem.at[layer, who, piece],
            device_id=device,
            device_id_type=MESH,
        )

    def arrive(layer, who, piece):
        pltpu.make_async_remote_copy(
            src_ref=slot(layer, who, piece),
            dst_ref=slot(layer, who, piece),
            send_sem=send_sem.at[layer, 0, piece, RING],
            recv_sem=recv_sem.at[layer, who, piece],
            device_id=(section, sibling),
            device_id_type=MESH,
        ).wait_recv()

    def small(index):
        return pltpu.make_async_remote_copy(
            src_ref=(gain_ref, rows_ref)[index],
            dst_ref=(gains.at[0], rows_in)[index],
            send_sem=small_send.at[index],
            recv_sem=small_recv.at[index],
            device_id=(other, me),
            device_id_type=MESH,
        )

    @pl.when(section == 0)
    def _():
        small(0).start()
        small(1).start()
        send(0, 0, 2, ACROSS, True).start()
        for piece in range(3):
            send(0, 0, piece, RING, True).start()
        for piece in range(2):
            send(0, 0, piece, ACROSS, True).start()
        for piece in range(3):
            send(0, 0, piece, SIB, True).start()
        gains[0] = gain_ref[...]
        weights[0, me] = w_ref[...]
        own = pltpu.make_async_copy(rows_ref, rows.at[0], local_sem.at[0])
        own.start()
        own.wait()

    @pl.when(section == 1)
    def _():
        for piece in range(3):
            send(1, 0, piece, RING, True).start()
        for piece in range(3):
            send(1, 0, piece, SIB, True).start()
        gains[1] = gain_ref[...]
        weights[1, me] = w_ref[...]
        own = pltpu.make_async_copy(rows_ref, rows.at[1], local_sem.at[0])
        own.start()
        small(0).wait_recv()
        small(1).wait_recv()
        own.wait()
        first = pltpu.make_async_copy(rows_in, rows.at[0], local_sem.at[1])
        first.start()
        first.wait()
        arrive(0, me, 2)
        send(0, 0, 2, RING).start()
        send(0, 0, 2, SIB).start()

    low = lax.broadcasted_iota(jnp.int32, (tokens, LANES), 1) < BLK
    low_w = lax.broadcasted_iota(jnp.int32, (LANES, LANES), 1) < BLK

    def both(target, tile, value):
        target[2 * tile] = value.astype(jnp.bfloat16)
        target[2 * tile + 1] = pltpu.roll(value, BLK, 1).astype(jnp.bfloat16)

    def norm(layer, source):
        def square(tile, total):
            wide = source[:, pl.ds(pl.multiple_of(tile * LANES, LANES), LANES)].astype(jnp.float32)
            return total + wide * wide

        total = lax.fori_loop(0, tiles, square, jnp.zeros((tokens, LANES), jnp.float32))
        mean = jnp.sum(total, axis=1, keepdims=True) * (1.0 / width)
        scale_ref[...] = jnp.broadcast_to(lax.rsqrt(mean + 1e-05), (tokens, LANES))

        def apply(tile, _):
            columns = pl.ds(pl.multiple_of(tile * LANES, LANES), LANES)
            wide = source[:, columns].astype(jnp.float32)
            both(blocks_in, tile, wide * scale_ref[...] * gains[layer, :, columns])
            return 0

        lax.fori_loop(0, tiles, apply, 0, unroll=2)

    def product(layer, source, base, pair, who, local):
        picked, kernels = [], []
        value = weights[layer, who, local]
        zero = jnp.zeros_like(value)
        for half in range(2):
            place_a = base + pair * 4 + half * 2
            index_a = rows[layer, place_a // 128, place_a % 128]
            index_b = rows[layer, (place_a + 1) // 128, (place_a + 1) % 128]
            picked.append(jnp.where(low, source[index_a], source[index_b]))
            kernels.append(jnp.where(low_w, value, zero) if half == 0 else jnp.where(low_w, zero, value))
        return jnp.dot(
            jnp.concatenate(picked, axis=1),
            jnp.concatenate(kernels, axis=0),
            preferred_element_type=jnp.float32,
        )

    def up(layer, who):
        def one(local, _):
            pair = who * ups + local
            sums = product(layer, blocks_in, 0, pair, who, local)
            both(blocks_hid, pair, jax.nn.gelu(sums, approximate=True))
            return 0

        lax.fori_loop(0, ups, one, 0, unroll=2)

    def down(layer, source):
        def one(who, _):
            for local in range(part):
                tile = who * part + local
                sums = product(layer, blocks_hid, 4 * ups * 2 * chips, tile, who, ups + local)
                columns = pl.ds(pl.multiple_of(tile * LANES, LANES), LANES)
                wide = source[:, columns].astype(jnp.float32)
                out_ref[:, columns] = (wide + keep_ref[...] * sums).astype(jnp.bfloat16)
            return 0

        lax.fori_loop(0, 2 * chips, one, 0)

    norm(0, x_ref)

    def step(s, _):
        @pl.when(section == 0)
        def _():
            @pl.when(s > 0)
            def _():
                for piece in range(3):
                    arrive(0, origin(s), piece)

                    @pl.when(s < chips - 1)
                    def _():
                        send(0, s, piece, RING).start()

                    if piece < 2:
                        send(0, s, piece, ACROSS).start()
                    send(0, s, piece, SIB).start()

        @pl.when(section == 1)
        def _():
            @pl.when(s > 0)
            def _():
                for layer, piece in ((1, 0), (1, 1), (1, 2), (0, 2)):
                    arrive(layer, origin(s), piece)

                    @pl.when(s < chips - 1)
                    def _():
                        send(layer, s, piece, RING).start()

                    send(layer, s, piece, SIB).start()

            for piece in range(2):
                arrive(0, origin(s), piece)
                send(0, s, piece, SIB).start()

        up(0, origin(s))

        @pl.when(s > 0)
        def _():
            for piece in range(2):
                arrive(0, origin_sib(s - 1), piece)
            up(0, origin_sib(s - 1))

        return 0

    lax.fori_loop(0, chips, step, 0)
    for piece in range(2):
        arrive(0, origin_sib(chips - 1), piece)
    up(0, origin_sib(chips - 1))

    def rest(s, _):
        arrive(0, origin_sib(s), 2)
        return 0

    lax.fori_loop(0, chips, rest, 0)
    down(0, x_ref)

    @pl.when(section == 1)
    def _():
        norm(1, out_ref)

        def one(s, _):
            for piece in range(3):
                arrive(1, origin_sib(s), piece)
            up(1, origin(s))
            up(1, origin_sib(s))
            return 0

        lax.fori_loop(0, chips, one, 0)
        down(1, out_ref)

    def finish(s, _):
        @pl.when(section == 0)
        def _():
            for piece in range(3):
                @pl.when(s < chips - 1)
                def _():
                    send(0, s, piece, RING).wait_send()

                if piece < 2:
                    send(0, s, piece, ACROSS).wait_send()
                send(0, s, piece, SIB).wait_send()

        @pl.when(section == 1)
        def _():
            for layer, piece in ((1, 0), (1, 1), (1, 2), (0, 2)):
                @pl.when(s < chips - 1)
                def _():
                    send(layer, s, piece, RING).wait_send()

                send(layer, s, piece, SIB).wait_send()
            for piece in range(2):
                send(0, s, piece, SIB).wait_send()

        return 0

    lax.fori_loop(0, chips, finish, 0)

    @pl.when(section == 0)
    def _():
        send(0, 0, 2, ACROSS).wait_send()
        small(0).wait_send()
        small(1).wait_send()


def paired(values, count):
    pairs = values.shape[0] // 4
    return values.reshape(pairs, 2, LANES, BLK).transpose(0, 2, 1, 3).reshape(pairs, LANES, LANES)


def flat_rows(index, depth):
    return jnp.stack([index[:, 0], index[:, 1] ^ 1], axis=1).reshape(-1)


def per_device_fused(activations, keep, gains, up_rows, up_blocks, down_rows, down_blocks):
    tokens, width = activations.shape
    devices = lax.axis_size("fsdp")
    own = jnp.concatenate([paired(up_blocks[0], UP_DEPTH), paired(down_blocks[0], DOWN_DEPTH)], axis=0)
    table = jnp.concatenate([flat_rows(up_rows[0], UP_DEPTH), flat_rows(down_rows[0], DOWN_DEPTH)])
    table = jnp.pad(table, (0, 1024 - table.shape[0])).reshape(8, 128)
    keep_wide = jnp.broadcast_to(keep.astype(jnp.float32)[:, None], (tokens, LANES))
    vmem = pl.BlockSpec(memory_space=pltpu.VMEM)
    result = pl.pallas_call(
        functools.partial(kernel, devices // 2),
        out_shape=jax.ShapeDtypeStruct((tokens, width), jnp.bfloat16),
        in_specs=[vmem] * 5,
        out_specs=vmem,
        scratch_shapes=[
            pltpu.VMEM((2, devices) + own.shape, jnp.bfloat16),
            pltpu.VMEM((width // BLK, tokens, LANES), jnp.bfloat16),
            pltpu.VMEM((up_rows.shape[1], tokens, LANES), jnp.bfloat16),
            pltpu.VMEM((tokens, LANES), jnp.float32),
            pltpu.VMEM((2, 1, width), jnp.float32),
            pltpu.VMEM((8, 128), jnp.int32),
            pltpu.SMEM((2, 8, 128), jnp.int32),
            pltpu.SemaphoreType.DMA((2, devices // 2, 3, 3)),
            pltpu.SemaphoreType.DMA((2, devices, 3)),
            pltpu.SemaphoreType.DMA((2,)),
            pltpu.SemaphoreType.DMA((2,)),
            pltpu.SemaphoreType.DMA((2,)),
        ],
        compiler_params=pltpu.CompilerParams(
            collective_id=0, has_side_effects=True, vmem_limit_bytes=48 * 1024 * 1024
        ),
    )(activations, keep_wide, gains.astype(jnp.float32), table, own)
    return result[None]


def solution(mesh):
    fused = mesh.shape["section"] == 2 and mesh.shape["fsdp"] == 16
    return jax.shard_map(
        per_device_fused if fused else per_device,
        mesh=mesh,
        in_specs=(
            P("fsdp", None),
            P("fsdp"),
            P("section", None),
            P("section", None, None),
            P("section", "fsdp", None),
            P("section", None, None),
            P("section", "fsdp", None),
        ),
        out_specs=P("section", "fsdp", None),
        check_vma=False,
    )
```

```python
import functools
import jax
import jax.numpy as jnp
from jax import lax
from jax.experimental import pallas as pl
from jax.experimental.pallas import tpu as pltpu
from jax.sharding import PartitionSpec as P

BLK = 64
UP_DEPTH = 2
DOWN_DEPTH = 2


def project(source, index, weights):
    count = source.shape[0]

    def one(column, sums):
        first = lax.dynamic_slice_in_dim(source, index[2 * column] * BLK, BLK, 1)
        second = lax.dynamic_slice_in_dim(source, index[2 * column + 1] * BLK, BLK, 1)
        part = jnp.dot(
            jnp.concatenate([first, second], axis=1),
            lax.dynamic_index_in_dim(weights, column, 0, keepdims=False),
            preferred_element_type=jnp.float32,
        )
        return lax.dynamic_update_slice_in_dim(sums, part, column * BLK, 1)

    columns = weights.shape[0]
    return lax.fori_loop(0, columns, one, jnp.zeros((count, columns * BLK), jnp.float32))


def per_device(activations, keep, gains, up_rows, up_blocks, down_rows, down_blocks):
    up_all = lax.all_gather(up_blocks[0], "fsdp", axis=0, tiled=True)
    down_all = lax.all_gather(down_blocks[0], "fsdp", axis=0, tiled=True)
    weights_up = up_all.reshape(-1, UP_DEPTH * BLK, BLK)
    weights_down = down_all.reshape(-1, DOWN_DEPTH * BLK, BLK)
    gain_wide = gains[0].astype(jnp.float32)
    keep_wide = keep.astype(jnp.float32)[:, None]
    section = lax.axis_index("section")
    sections = lax.axis_size("section")

    def turn_step(turn, carry):
        held, record = carry
        wide = held.astype(jnp.float32)
        meansq = jnp.mean(wide * wide, axis=-1, keepdims=True)
        normed = (wide * lax.rsqrt(meansq + 1e-05) * gain_wide).astype(jnp.bfloat16)
        up_sums = project(normed, up_rows[0].reshape(-1), weights_up)
        hidden = jax.nn.gelu(up_sums, approximate=True).astype(jnp.bfloat16)
        down_sums = project(hidden, down_rows[0].reshape(-1), weights_down)
        result = (wide + keep_wide * down_sums).astype(jnp.bfloat16)
        record = jnp.where(section == turn, result, record)
        pairs = [(source, source + 1) for source in range(sections - 1)]
        return lax.ppermute(result, "section", pairs), record

    return lax.fori_loop(0, sections, turn_step, (activations, activations))[1][None]


LANES = 2 * BLK
MESH = pl.DeviceIdType.MESH
RING, SIB, ACROSS = 0, 1, 2


def kernel(
    chips,
    x_ref,
    keep_row,
    gain_ref,
    rows_ref,
    w_ref,
    out_ref,
    weights,
    blocks_in,
    blocks_hid,
    scale_ref,
    keep_ref,
    gains,
    rows_in,
    rows,
    send_sem,
    recv_sem,
    small_send,
    small_recv,
    local_sem,
):
    section = lax.axis_index("section")
    me = lax.axis_index("fsdp")
    core = me % 2
    chip = me // 2
    depth_z = chips // 2
    y = chip % 2
    z = chip // 2
    place = z * (1 - y) + (chips - 1 - z) * y
    step_dir = 1 - 2 * core

    def at(position, which):
        position = (position + 2 * chips) % chips
        back = position // depth_z
        zz = position * (1 - back) + (chips - 1 - position) * back
        return (zz * 2 + back) * 2 + which

    ahead = at(place + step_dir, core)
    behind = at(place - step_dir, core)
    sibling = me + 1 - 2 * core
    other = 1 - section
    tokens, width = x_ref.shape
    tiles = width // LANES
    ups = 6 * w_ref.shape[0] // 9
    part = w_ref.shape[0] // 3

    barrier = pltpu.get_barrier_semaphore()
    for device in ((section, ahead), (section, behind), (section, sibling), (other, me)):
        pl.semaphore_signal(barrier, inc=1, device_id=device, device_id_type=MESH)
    pl.semaphore_wait(barrier, 4)

    def origin(step):
        return at(place - step_dir * step, core)

    def origin_sib(step):
        return at(place + step_dir * step, 1 - core)

    def slot(layer, who, piece):
        return weights.at[layer, who, pl.ds(piece * part, part)]

    def send(layer, step, piece, way, own=False):
        who = origin(step)
        device = ((section, ahead), (section, sibling), (other, me))[way]
        return pltpu.make_async_remote_copy(
            src_ref=w_ref.at[pl.ds(piece * part, part)] if own else slot(layer, who, piece),
            dst_ref=slot(layer, who, piece),
            send_sem=send_sem.at[layer, step, piece, way],
            recv_sem=recv_sem.at[layer, who, piece],
            device_id=device,
            device_id_type=MESH,
        )

    def arrive(layer, who, piece):
        pltpu.make_async_remote_copy(
            src_ref=slot(layer, who, piece),
            dst_ref=slot(layer, who, piece),
            send_sem=send_sem.at[layer, 0, piece, RING],
            recv_sem=recv_sem.at[layer, who, piece],
            device_id=(section, sibling),
            device_id_type=MESH,
        ).wait_recv()

    def small(index):
        return pltpu.make_async_remote_copy(
            src_ref=(gains.at[0], rows_ref)[index],
            dst_ref=(gains.at[0], rows_in)[index],
            send_sem=small_send.at[index],
            recv_sem=small_recv.at[index],
            device_id=(other, me),
            device_id_type=MESH,
        )

    @pl.when(section == 0)
    def _():
        gains[0] = gain_ref[...].astype(jnp.float32)
        small(0).start()
        small(1).start()
        send(0, 0, 2, ACROSS, True).start()
        for piece in range(3):
            send(0, 0, piece, RING, True).start()
        for piece in range(2):
            send(0, 0, piece, ACROSS, True).start()
        for piece in range(3):
            send(0, 0, piece, SIB, True).start()
        weights[0, me] = w_ref[...]
        own = pltpu.make_async_copy(rows_ref, rows.at[0], local_sem.at[0])
        own.start()
        own.wait()

    @pl.when(section == 1)
    def _():
        for piece in range(3):
            send(1, 0, piece, RING, True).start()
        for piece in range(3):
            send(1, 0, piece, SIB, True).start()
        gains[1] = gain_ref[...].astype(jnp.float32)
        weights[1, me] = w_ref[...]
        own = pltpu.make_async_copy(rows_ref, rows.at[1], local_sem.at[0])
        own.start()
        small(0).wait_recv()
        small(1).wait_recv()
        own.wait()
        first = pltpu.make_async_copy(rows_in, rows.at[0], local_sem.at[1])
        first.start()
        first.wait()
        arrive(0, me, 2)
        send(0, 0, 2, RING).start()
        send(0, 0, 2, SIB).start()

    low = lax.broadcasted_iota(jnp.int32, (16, LANES), 1) < BLK

    def merge(first, second):
        shape = (first.shape[0] // 16, 16, LANES)
        return jnp.where(low[None], first.reshape(shape), second.reshape(shape)).reshape(first.shape)


    def gelu(value):
        inner = value * (0.7978845608028654 + 0.035677408136300125 * (value * value))
        scaled = 0.5 * value
        return scaled + scaled * jnp.tanh(inner)

    def both(target, tile, value):
        rounded = value.astype(jnp.bfloat16)
        target[2 * tile] = rounded
        target[2 * tile + 1] = jnp.concatenate([rounded[:, BLK:], rounded[:, :BLK]], axis=1)

    def norm(layer, source):
        def square(tile, total):
            wide = source[:, pl.ds(pl.multiple_of(tile * LANES, LANES), LANES)].astype(jnp.float32)
            return total + wide * wide

        total = lax.fori_loop(0, tiles, square, jnp.zeros((tokens, LANES), jnp.float32), unroll=8)
        mean = jnp.sum(total, axis=1, keepdims=True) * (1.0 / width)
        scale_ref[...] = jnp.broadcast_to(lax.rsqrt(mean + 1e-05), (tokens, LANES))

        def apply(tile, _):
            columns = pl.ds(pl.multiple_of(tile * LANES, LANES), LANES)
            wide = source[:, columns].astype(jnp.float32)
            both(blocks_in, tile, wide * scale_ref[...] * gains[layer, :, columns])
            return 0

        lax.fori_loop(0, tiles, apply, 0, unroll=8)

    def product(layer, source, base, pair, who, local):
        picked, kernels = [], []
        value = weights[layer, who, local]
        zero = jnp.zeros_like(value)
        for half in range(2):
            place_a = base + pair * 4 + half * 2
            index_a = rows[layer, place_a // 128, place_a % 128]
            index_b = rows[layer, (place_a + 1) // 128, (place_a + 1) % 128] ^ 1
            picked.append(merge(source[index_a], source[index_b]))
            kernels.append(merge(value, zero) if half == 0 else merge(zero, value))
        return jnp.dot(
            jnp.concatenate(picked, axis=1),
            jnp.concatenate(kernels, axis=0),
            preferred_element_type=jnp.float32,
        )

    def up(layer, who):
        def one(local, _):
            pair = who * ups + local
            sums = product(layer, blocks_in, 0, pair, who, local)
            both(blocks_hid, pair, gelu(sums))
            return 0

        lax.fori_loop(0, ups, one, 0, unroll=6)

    def down(layer, source):
        def one(who, _):
            for local in range(part):
                tile = who * part + local
                sums = product(layer, blocks_hid, 4 * ups * 2 * chips, tile, who, ups + local)
                columns = pl.ds(pl.multiple_of(tile * LANES, LANES), LANES)
                wide = source[:, columns].astype(jnp.float32)
                out_ref[:, columns] = (wide + keep_ref[...] * sums).astype(jnp.bfloat16)
            return 0

        lax.fori_loop(0, 2 * chips, one, 0, unroll=4)

    same = lax.broadcasted_iota(jnp.int32, (tokens, tokens), 0) == lax.broadcasted_iota(
        jnp.int32, (tokens, tokens), 1
    )
    kept = jnp.sum(jnp.where(same, keep_row[...].astype(jnp.float32), 0.0), axis=1, keepdims=True)
    keep_ref[...] = jnp.broadcast_to(kept, (tokens, LANES))
    norm(0, x_ref)

    def step(s, _):
        @pl.when(section == 0)
        def _():
            @pl.when(s > 0)
            def _():
                for piece in range(3):
                    arrive(0, origin(s), piece)

                    @pl.when(s < chips - 1)
                    def _():
                        send(0, s, piece, RING).start()

                    if piece < 2:
                        send(0, s, piece, ACROSS).start()
                    send(0, s, piece, SIB).start()

        @pl.when(section == 1)
        def _():
            @pl.when(s > 0)
            def _():
                for layer, piece in ((1, 0), (1, 1), (1, 2), (0, 2)):
                    arrive(layer, origin(s), piece)

                    @pl.when(s < chips - 1)
                    def _():
                        send(layer, s, piece, RING).start()

                    send(layer, s, piece, SIB).start()

            for piece in range(2):
                arrive(0, origin(s), piece)
                send(0, s, piece, SIB).start()

        up(0, origin(s))

        @pl.when(s > 0)
        def _():
            for piece in range(2):
                arrive(0, origin_sib(s - 1), piece)
            up(0, origin_sib(s - 1))

        return 0

    lax.fori_loop(0, chips, step, 0)
    for piece in range(2):
        arrive(0, origin_sib(chips - 1), piece)
    up(0, origin_sib(chips - 1))

    def rest(s, _):
        arrive(0, origin_sib(s), 2)
        return 0

    lax.fori_loop(0, chips, rest, 0)
    down(0, x_ref)

    @pl.when(section == 1)
    def _():
        norm(1, out_ref)

        def one(s, _):
            for piece in range(3):
                arrive(1, origin_sib(s), piece)
            up(1, origin(s))
            up(1, origin_sib(s))
            return 0

        lax.fori_loop(0, chips, one, 0)
        down(1, out_ref)

    def finish(s, _):
        @pl.when(section == 0)
        def _():
            for piece in range(3):
                @pl.when(s < chips - 1)
                def _():
                    send(0, s, piece, RING).wait_send()

                if piece < 2:
                    send(0, s, piece, ACROSS).wait_send()
                send(0, s, piece, SIB).wait_send()

        @pl.when(section == 1)
        def _():
            for layer, piece in ((1, 0), (1, 1), (1, 2), (0, 2)):
                @pl.when(s < chips - 1)
                def _():
                    send(layer, s, piece, RING).wait_send()

                send(layer, s, piece, SIB).wait_send()
            for piece in range(2):
                send(0, s, piece, SIB).wait_send()

        return 0

    lax.fori_loop(0, chips, finish, 0)

    @pl.when(section == 0)
    def _():
        send(0, 0, 2, ACROSS).wait_send()
        small(0).wait_send()
        small(1).wait_send()


def paired(values):
    pairs = values.shape[0] // 4
    return values.reshape(pairs, 2, LANES, BLK).transpose(0, 2, 1, 3).reshape(pairs, LANES, LANES)


def per_device_fused(activations, keep, gains, up_rows, up_blocks, down_rows, down_blocks):
    tokens, width = activations.shape
    devices = lax.axis_size("fsdp")
    own = paired(jnp.concatenate([up_blocks[0], down_blocks[0]], axis=0))
    table = jnp.concatenate([up_rows[0].reshape(-1), down_rows[0].reshape(-1)])
    table = jnp.pad(table, (0, 1024 - table.shape[0])).reshape(8, 128)
    vmem = pl.BlockSpec(memory_space=pltpu.VMEM)
    result = pl.pallas_call(
        functools.partial(kernel, devices // 2),
        out_shape=jax.ShapeDtypeStruct((tokens, width), jnp.bfloat16),
        in_specs=[vmem] * 5,
        out_specs=vmem,
        scratch_shapes=[
            pltpu.VMEM((2, devices) + own.shape, jnp.bfloat16),
            pltpu.VMEM((width // BLK, tokens, LANES), jnp.bfloat16),
            pltpu.VMEM((up_rows.shape[1], tokens, LANES), jnp.bfloat16),
            pltpu.VMEM((tokens, LANES), jnp.float32),
            pltpu.VMEM((tokens, LANES), jnp.float32),
            pltpu.VMEM((2, 1, width), jnp.float32),
            pltpu.VMEM((8, 128), jnp.int32),
            pltpu.SMEM((2, 8, 128), jnp.int32),
            pltpu.SemaphoreType.DMA((2, devices // 2, 3, 3)),
            pltpu.SemaphoreType.DMA((2, devices, 3)),
            pltpu.SemaphoreType.DMA((2,)),
            pltpu.SemaphoreType.DMA((2,)),
            pltpu.SemaphoreType.DMA((2,)),
        ],
        compiler_params=pltpu.CompilerParams(
            collective_id=0, has_side_effects=True, vmem_limit_bytes=48 * 1024 * 1024
        ),
    )(activations, keep[None], gains, table, own)
    return result[None]


def solution(mesh):
    fused = mesh.shape["section"] == 2 and mesh.shape["fsdp"] == 16
    return jax.shard_map(
        per_device_fused if fused else per_device,
        mesh=mesh,
        in_specs=(
            P("fsdp", None),
            P("fsdp"),
            P("section", None),
            P("section", None, None),
            P("section", "fsdp", None),
            P("section", None, None),
            P("section", "fsdp", None),
        ),
        out_specs=P("section", "fsdp", None),
        check_vma=False,
    )
```
